512 devices in a mesh: gx: 16 (over z), gy: 32 (over y, x, core).
Axes of the slice: x: 4, y: 4, z: 16, core: 2. Of those that a mesh axis runs over, the one named last changes fastest.
Arguments:
- permeability: float32 [32, 512, 2048], P(None, 'gy', 'gx'), may hold values from 0.25 to 4
- source: float32 [32, 512, 2048], P(None, 'gy', 'gx'), may hold values from -16 to 16
- phase_mask: int32 [32, 512, 2048], P(None, 'gy', 'gx'), may hold values from 0 to 2
Outputs:
- pressure: float32 [32, 512, 2048], P(None, 'gy', 'gx')
- correction_mid: float32 [16, 256, 1024], P(None, 'gy', 'gx')
- correction_low: float32 [8, 128, 512], P(None, 'gy', 'gx')
The draws below stay inside these ranges and needn't reach their ends.
Inputs may be any that keep to these rules, and one draw needn't show every extreme that they name: `phase_mask`: 0 liquid, 1 mushy, 2 solid.
All inputs are finite; a program needn't handle non-finite values.
Results may differ from the reference program's by a relative error of at most 0.0003.
Values sent between devices are 32-bit elements; how exact they have to be, the bound alone decides.
A program may use at most 128 MiB of HBM per device.

```python
import math
import jax
import jax.numpy as jnp

NZ = 32
NU = 8
COARSE_SWEEPS = 8
NX = 2048
NY = 512


def touch_ends(values, stream_key, low, largest):
    spot = [jax.random.randint(jax.random.fold_in(stream_key, axis), (), 0, length) for axis, length in enumerate(values.shape)]
    longest = values.shape.index(max(values.shape))
    next_to = spot[:longest] + [(spot[longest] + 1) % values.shape[longest]] + spot[longest + 1:]
    return values.at[tuple(spot)].set(low).at[tuple(next_to)].set(largest)


def level_of(key, dims, cuts, smallest, largest):
    gain = 1.0
    for position, blocks in cuts:
        steps = jax.random.uniform(jax.random.fold_in(jax.random.fold_in(key, 6), position), (blocks,), jnp.float32, smallest / len(cuts), largest / len(cuts))
        gain = gain * jnp.repeat(jnp.exp(steps), dims[position] // blocks).reshape((-1,) + (1,) * (len(dims) - 1 - position))
    return gain


def centred(stream_key, shape, spread, limit, cuts=(), dtype=jnp.bfloat16):
    drawn = jax.random.normal(stream_key, shape, jnp.float32) * spread
    if len(cuts) > 0:
        drawn = level_of(stream_key, shape, cuts, -0.22, 0.18) * drawn
    return jnp.clip(drawn, min=-limit, max=limit).astype(dtype)


def setup_inputs(seed: int = 0) -> dict:
    splits = jax.random.split(jax.random.key(seed), 4)
    permeability = jnp.clip(jnp.exp(math.log(4.0) - 2.7725887 * jax.random.uniform(splits[0], (NZ, NY, NX), jnp.float32) ** level_of(splits[0], (NZ, NY, NX), ((1, 32), (2, 16)), -0.2, 0.2)), 0.25, 4.0)
    source = centred(splits[1], (NZ, NY, NX), 4.0, 16.0, ((1, 32), (2, 16)), jnp.float32)
    phase_mask = touch_ends(jax.random.randint(splits[2], (NZ, NY, NX), 0, 3), jax.random.fold_in(splits[2], 1), 0, 2).astype(jnp.int32)
    return dict(permeability=permeability, source=source, phase_mask=phase_mask)


RELAXATION = 0.8
STORAGE = 0.05
LEAK_SHARE = 0.1


def harmonic(lower_cell, upper_cell):
    face_sum = lower_cell + upper_cell
    divisor = jnp.where(face_sum > 0.0, face_sum, 1.0)
    return 2.0 * lower_cell * upper_cell / divisor


def coefficients(conductance, face_scale, store_scale):
    padded = jnp.pad(conductance, 1)
    east_west = harmonic(padded[1:-1, 1:-1, :-1], padded[1:-1, 1:-1, 1:]) * face_scale
    north_south = harmonic(padded[1:-1, :-1, 1:-1], padded[1:-1, 1:, 1:-1]) * face_scale
    vertical = harmonic(padded[:-1, 1:-1, 1:-1], padded[1:, 1:-1, 1:-1]) * face_scale
    diagonal = (east_west[:, :, 1:] + east_west[:, :, :-1] + north_south[:, 1:] + north_south[:, :-1]
                + vertical[1:] + vertical[:-1] + store_scale * conductance
                + jnp.where(conductance > 0.0, 0.0, 1.0))
    return east_west, north_south, vertical, diagonal


def operate(iterate, stencil):
    east_west, north_south, vertical, diagonal = stencil
    padded = jnp.pad(iterate, 1)
    return (diagonal * iterate
            - east_west[:, :, 1:] * padded[1:-1, 1:-1, 2:]
            - east_west[:, :, :-1] * padded[1:-1, 1:-1, :-2]
            - north_south[:, 1:] * padded[1:-1, 2:, 1:-1]
            - north_south[:, :-1] * padded[1:-1, :-2, 1:-1]
            - vertical[1:] * padded[2:, 1:-1, 1:-1]
            - vertical[:-1] * padded[:-2, 1:-1, 1:-1])


def smooth(right_side, stencil, sweeps):
    weight = RELAXATION / stencil[3]
    iterate = weight * right_side
    for sweep_no in range(sweeps - 1):
        iterate = iterate + weight * (right_side - operate(iterate, stencil))
    return iterate


def restrict(cells):
    depth_cells, row_cells, column_cells = cells.shape
    return cells.reshape(depth_cells // 2, 2, row_cells // 2, 2, column_cells // 2, 2).sum(axis=(1, 3, 5))


def reference(permeability, source, phase_mask):
    conductance = jnp.where(phase_mask == 2, 0.0, permeability)
    right_side = jnp.where(phase_mask == 1, source, 0.0)
    stencil = coefficients(conductance, 1.0, STORAGE)
    pressure = smooth(right_side, stencil, NU)
    side_mid = restrict(right_side - operate(pressure, stencil))
    cond_mid = restrict(LEAK_SHARE * permeability + (1.0 - LEAK_SHARE) * conductance) * 0.125
    stencil_mid = coefficients(cond_mid, 2.0, 8.0 * STORAGE)
    correction_mid = smooth(side_mid, stencil_mid, NU)
    side_low = restrict(side_mid - operate(correction_mid, stencil_mid))
    cond_low = restrict(cond_mid) * 0.125
    stencil_low = coefficients(cond_low, 4.0, 64.0 * STORAGE)
    correction_low = smooth(side_low, stencil_low, COARSE_SWEEPS)
    return pressure, correction_mid, correction_low
```

```python
import functools

import jax
import jax.numpy as jnp
from jax import lax
from jax.experimental import pallas as pl
from jax.experimental.pallas import tpu as pltpu
from jax.sharding import PartitionSpec as P

MESH = pl.DeviceIdType.MESH
F32 = jnp.float32
STORAGE = 0.05
LEAK = 0.1
TINY = 1e-30

HALO = 9
ROWS = 16 + 2 * HALO
MID = 24
LOW = 20
MX = 22
LX = 11


def rcp(d):
    r = pl.reciprocal(d, approx=True)
    return r * (2.0 - d * r)


def harm(a, b):
    return (2.0 * a * b) * rcp(jnp.maximum(a + b, TINY))


def lane_of(shape):
    return lax.broadcasted_iota(jnp.int32, shape, len(shape) - 1)


def sub_of(shape):
    return lax.broadcasted_iota(jnp.int32, shape, len(shape) - 2)


def roll(x, shift):
    shift = shift % 128
    return x if shift == 0 else pltpu.roll(x, shift, x.ndim - 1)


def east(x):
    return roll(x, 127)


def west(x):
    return roll(x, 1)


def up(x):
    return pltpu.roll(x, 7, x.ndim - 2)


def down(x):
    return pltpu.roll(x, 1, x.ndim - 2)


def strip_up(x):
    y = roll(x, 96)
    return jnp.where(lane_of(x.shape) >= 96, up(y), y)


def strip_down(x):
    y = roll(x, 32)
    return jnp.where(lane_of(x.shape) < 32, down(y), y)


def groups(parts, shifts):
    lane = lane_of(parts[0].shape)
    out = roll(parts[3], shifts[3])
    for q in (2, 1, 0):
        out = jnp.where(lane < 32 * (q + 1), roll(parts[q], shifts[q]), out)
    return out


def pack_west(m):
    return groups(m, [32 * k + 9 for k in range(4)])


def pack_east(m):
    return groups(m, [32 * k + 23 for k in range(4)])


def main_east(m, k, strip):
    ins = roll(strip, 104 - 32 * k)
    return jnp.where(lane_of(m.shape) == 127, ins, east(m))


def main_west(m, k, strip):
    ins = roll(strip, -(32 * k + 8))
    return jnp.where(lane_of(m.shape) == 0, ins, west(m))


def finish(t, c, store):
    total = t[0]
    for x in t[1:]:
        total = total + x
    return total + store * c + jnp.where(c > 0.0, 0.0, 1.0)


def kernel(ngx, ngy, perm, source, mask, out_fine, out_mid, out_low,
           cm, bm, sr, sl, rl, rr, cs, cse, csw, coef, inv, v,
           cmx, cmid, midx, mrl, mrr, mcoef, mvx, mv, clow, lcoef, lvx, lv, tmid, tlow, send, recv):
    gx, gy = lax.axis_index("gx"), lax.axis_index("gy")

    def dev(dx, dy):
        return (lax.rem(gx + dx + ngx, ngx), lax.rem(gy + dy + 2 * ngy, ngy))

    around = [(dx, dy) for dx in (-1, 0, 1) for dy in (-1, 0, 1) if (dx, dy) != (0, 0)]
    partners = around + [(0, -2), (0, 2)]
    barrier = pltpu.get_barrier_semaphore()
    for d in partners:
        pl.semaphore_signal(barrier, inc=1, device_id=dev(*d), device_id_type=MESH)

    made = [0]

    def copy(src, dst, to):
        i = made[0]
        made[0] += 1
        return pltpu.make_async_remote_copy(
            src_ref=src, dst_ref=dst, send_sem=send.at[i], recv_sem=recv.at[i],
            device_id=dev(*to), device_id_type=MESH)


    def take(ref, y, k):
        return ref[pl.ds(k * 16 + y, 8, stride=64), :]

    lane = lane_of((8, 128))
    sub = sub_of((8, 128))
    pair_mid = jnp.clip(2 * (lane - MX), 0, 127)
    pair_low = jnp.clip(2 * lane, 0, 127)

    def compact(x, index):
        return jnp.take_along_axis(x + east(x), index, axis=1, mode="promise_in_bounds")

    def load_pair(i, carry):
        acc = [None, None]
        for o in range(2):
            y = 2 * i + o
            conds, rights = [], []
            for k in range(4):
                p, m = take(perm, y, k), take(mask, y, k)
                c = jnp.where(m == 2, 0.0, p)
                b = jnp.where(m == 1, take(source, y, k), 0.0)
                cm[HALO + y, k] = c
                bm[HALO + y, k] = b
                conds.append(c)
                rights.append(b)
                term = LEAK * p + (1.0 - LEAK) * c
                acc[k // 2] = term if acc[k // 2] is None else acc[k // 2] + term
            aw, ae = pack_west(conds), pack_east(conds)
            bw, be = pack_west(rights), pack_east(rights)
            c32 = jnp.bitwise_and(lane, 31)
            sr[y] = jnp.where(c32 < 16, aw, roll(bw, 16))
            sl[y] = jnp.where(c32 >= 16, ae, roll(be, 112))
        for k in range(2):
            cmx[8 + i, k] = compact(acc[k], pair_mid) * 0.125
        return carry

    lax.fori_loop(0, 8, load_pair, 0)

    def mid_pack(src, row0, slot):
        for i in range(4):
            parts = [src[row0 + i + 4 * (q // 2), q % 2] for q in range(4)]
            midx[slot, 0, i] = groups(parts, [32 * q - (MX + 42) for q in range(4)])
            midx[slot, 1, i] = groups(parts, [32 * q - MX for q in range(4)])

    mid_pack(cmx, 8, 0)
    pl.semaphore_wait(barrier, len(partners))

    def start(cs_):
        for c_ in cs_:
            c_.start()

    def arrive(cs_):
        for c_ in cs_:
            c_.wait_recv()

    def strips(src_r, src_l, dst_l, dst_r, n):
        own = src_r.shape[0]
        got = []
        for dx, src, dst in ((1, src_r, dst_l), (-1, src_l, dst_r)):
            got.append(copy(src, dst.at[pl.ds(n, own)], (dx, 0)))
            got.append(copy(src.at[pl.ds(own - n, n)], dst.at[pl.ds(0, n)], (dx, 1)))
            got.append(copy(src.at[pl.ds(0, n)], dst.at[pl.ds(n + own, n)], (dx, -1)))
        return got

    def edges(buf, n, own, first=0):
        return [copy(buf.at[pl.ds(first + own, n)], buf.at[pl.ds(first, n)], (0, 1)),
                copy(buf.at[pl.ds(first + n, n)], buf.at[pl.ds(first + n + own, n)], (0, -1))]

    cond_y = edges(cm, HALO, 16)
    raw_x = strips(sr, sl, rl, rr, HALO)
    right_y = edges(bm, HALO, 16)
    start(cond_y + raw_x + right_y)

    def mid_exchange(buf, slot):
        got = edges(buf, 8, 8)
        for dx, side, dst in ((1, 0, mrl), (-1, 1, mrr)):
            src = midx.at[slot, side]
            for dy, block in ((0, 1), (1, 0), (-1, 2)):
                got.append(copy(src, dst.at[slot, block], (dx, dy)))
        return got

    cond_mid = mid_exchange(cmx, 0)
    start(cond_mid)

    arrive(cond_y + raw_x)

    @pl.when(gy == 0)
    def _():
        cm[pl.ds(0, HALO)] = jnp.zeros((HALO, 4, 8, 128), F32)

    @pl.when(gy == ngy - 1)
    def _():
        cm[pl.ds(16 + HALO, HALO)] = jnp.zeros((HALO, 4, 8, 128), F32)

    c32 = jnp.bitwise_and(lane, 31)
    inside = jnp.where(gx == 0, 9, 0), jnp.where(gx == ngx - 1, 23, 32)
    keep = (c32 >= inside[0]) & (c32 < inside[1])

    def strip_row(r, carry):
        parts = [cm[r, k] for k in range(4)]
        aw, ae = pack_west(parts), pack_east(parts)
        live = jnp.where(((gy == 0) & (r < HALO)) | ((gy == ngy - 1) & (r >= HALO + 16)), 0.0, 1.0)
        c = jnp.where(c32 < 9, rl[r], jnp.where(c32 < 16, aw, jnp.where(c32 < 23, ae, rr[r])))
        c = jnp.where(keep, c, 0.0) * live
        cs[r] = c
        cse[r] = east(jnp.where(c32 == 16, aw, c))
        csw[r] = west(jnp.where(c32 == 15, ae, c))
        return carry

    lax.fori_loop(0, ROWS, strip_row, 0, unroll=2)

    top = sub == 7

    def fine_coefs(i, carry):
        r = 1 + i
        m = [[cm[r + d, k] for k in range(4)] for d in (-1, 0, 1)]
        s = [cs[r + d] for d in (-1, 0, 1)]
        se = cse[r]
        c = s[1]
        te = harm(c, se)
        tw = harm(c, csw[r])
        tn, ts = harm(c, s[2]), harm(c, s[0])
        tu = harm(c, jnp.where(top & (lane >= 96), 0.0, strip_up(c)))
        faces = [te, tw, tn, ts, tu, strip_down(tu)]

        def put(k, faces, c):
            diag = finish(faces, c, STORAGE)
            w = 0.8 * rcp(diag)
            for f in range(6):
                coef[f, r, k] = w * faces[f]
            coef[6, r, k] = w
            inv[r, k] = 1.25 * diag

        put(4, faces, c)
        ups = [harm(m[1][k], m[1][k + 1]) for k in range(3)]
        ups.append(harm(m[1][3], jnp.where(top, 0.0, up(m[1][0]))))
        for k in range(4):
            c = m[1][k]
            e = harm(c, main_east(c, k, s[1]))
            w_ = main_west(e, k, te)
            d_ = ups[k - 1] if k else down(ups[3])
            put(k, [e, w_, harm(c, m[2][k]), harm(c, m[0][k]), ups[k], d_], c)
        return carry

    lax.fori_loop(0, ROWS - 2, fine_coefs, 0, unroll=2)

    arrive(right_y)
    for p in range(2):
        for r in (0, ROWS - 1):
            v[p, r] = jnp.zeros((5, 8, 128), F32)

    def first(i, carry):
        r = 1 + i
        parts = [bm[r, k] for k in range(4)]
        for k in range(4):
            v[0, r, k] = coef[6, r, k] * parts[k]
        aw, ae = pack_west(parts), pack_east(parts)
        b = jnp.where(c32 < 9, roll(rl[r], 112), jnp.where(c32 < 16, aw, jnp.where(c32 < 23, ae, roll(rr[r], 16))))
        x = coef[6, r, 4] * b
        v[0, r, 4] = x
        coef[6, r, 4] = x
        for k in range(4):
            coef[6, r, k] = v[0, r, k]
        return carry

    lax.fori_loop(0, ROWS - 2, first, 0, unroll=2)

    def sweep_main(p, r, k, x, x0, x2, strip):
        u = x[k + 1] if k < 3 else up(x[0])
        d = x[k - 1] if k else down(x[3])
        a = [coef[f, r, k] for f in range(7)]
        return (0.2 * x[k] + a[6] + a[0] * main_east(x[k], k, strip) + a[1] * main_west(x[k], k, strip)
                + a[2] * x2[k] + a[3] * x0[k] + a[4] * u + a[5] * d)

    def sweep(j, carry):
        p, half = lax.rem(j + 1, 2), lax.div(j, 2)
        q = 1 - p

        def block(i, carry):
            r0 = 1 + 2 * half + 4 * i
            rows = [[v[p, r0 + o - 1, k] for k in range(5)] for o in range(6)]
            for o in range(4):
                x0, x, x2 = rows[o], rows[o + 1], rows[o + 2]
                r = r0 + o
                new = []
                for k in range(4):
                    new.append(sweep_main(p, r, k, x, x0, x2, x[4]))
                s = x[4]
                a = [coef[f, r, 4] for f in range(7)]
                new.append(0.2 * s + a[6] + a[0] * east(s) + a[1] * west(s) + a[2] * x2[4] + a[3] * x0[4]
                           + a[4] * strip_up(s) + a[5] * strip_down(s))
                for k in range(5):
                    v[q, r, k] = new[k]
            return carry

        lax.fori_loop(0, 8 - half, block, 0)
        return carry

    lax.fori_loop(1, 8, sweep, 0)

    def mid_join(buf, slot, row):
        block, i = row // 8, row % 8
        out = []
        for k in range(2):
            q = 2 * (i // 4) + k
            left = roll(mrl[slot, block, i % 4], -32 * q)
            right = roll(mrr[slot, block, i % 4], MX + 64 - 32 * q)
            out.append(jnp.where(lane < MX, left, jnp.where(lane < MX + 64, buf[row, k], right)))
        return out

    arrive(cond_mid)
    lo, hi = jnp.where(gx == 0, MX, 0), jnp.where(gx == ngx - 1, MX + 64, 128)
    keep_mid = (lane >= lo) & (lane < hi)
    live = [jnp.where(gy == 0, 0.0, 1.0), 1.0, jnp.where(gy == ngy - 1, 0.0, 1.0)]
    for row in range(MID):
        joined = mid_join(cmx, 0, row)
        for k in range(2):
            c = jnp.where(keep_mid, joined[k], 0.0)
            cmid[row, k] = c if row // 8 == 1 else c * live[row // 8]

    def mid_coefs(i, carry):
        r = 1 + i
        x = [[cmid[r + d, k] for k in range(2)] for d in (-1, 0, 1)]
        u = [2.0 * harm(x[1][0], x[1][1]), 2.0 * harm(x[1][1], jnp.where(top, 0.0, up(x[1][0])))]
        for k in range(2):
            c = x[1][k]
            e = 2.0 * harm(c, east(c))
            faces = [e, west(e), 2.0 * harm(c, x[2][k]), 2.0 * harm(c, x[0][k]), u[k], u[0] if k else down(u[1])]
            diag = finish(faces, c, 8.0 * STORAGE)
            w = 0.8 * rcp(diag)
            for f in range(6):
                mcoef[f, r, k] = w * faces[f]
            mcoef[6, r, k] = w
            mcoef[7, r, k] = 1.25 * diag
        return carry

    lax.fori_loop(0, MID - 2, mid_coefs, 0, unroll=2)

    for i in range(4):
        acc = cmid[8 + 2 * i, 0] + cmid[8 + 2 * i, 1] + cmid[9 + 2 * i, 0] + cmid[9 + 2 * i, 1]
        clow[8 + i] = compact(acc, pair_low) * 0.125

    def low_exchange(buf):
        return [copy(buf.at[pl.ds(8, 4)], buf.at[pl.ds(4, 4)], (0, 1)),
                copy(buf.at[pl.ds(8, 4)], buf.at[pl.ds(12, 4)], (0, -1)),
                copy(buf.at[pl.ds(8, 4)], buf.at[pl.ds(0, 4)], (0, 2)),
                copy(buf.at[pl.ds(8, 4)], buf.at[pl.ds(16, 4)], (0, -2))]

    cond_low = low_exchange(clow)
    start(cond_low)

    def fine_residual(i, carry):
        acc = [None, None]
        r0 = HALO + 2 * i
        rows = [[v[1, r0 + o - 1, k] for k in range(4)] for o in range(4)]
        for o in range(2):
            r = r0 + o
            x0, x, x2 = rows[o], rows[o + 1], rows[o + 2]
            strip = v[1, r, 4]
            for k in range(4):
                res = (sweep_main(1, r, k, x, x0, x2, strip) - x[k]) * inv[r, k]
                acc[k // 2] = res if acc[k // 2] is None else acc[k // 2] + res
        for k in range(2):
            mvx[8 + i, k] = mcoef[6, 8 + i, k] * compact(acc[k], pair_mid)
        return carry

    lax.fori_loop(0, 8, fine_residual, 0)
    mid_pack(mvx, 8, 1)
    right_mid = mid_exchange(mvx, 1)
    start(right_mid)

    def write_fine(y, carry):
        for k in range(4):
            out_fine[pl.ds(k * 16 + y, 8, stride=64), :] = v[1, HALO + y, k]
        return carry

    lax.fori_loop(0, 16, write_fine, 0, unroll=4)

    arrive(cond_low)
    for row in list(range(1, 8)) + list(range(12, 19)):
        far = ngy - 1 - gy if row >= 12 else gy
        near = (row - 12) // 4 + 1 if row >= 12 else (11 - row) // 4
        clow[row] = clow[row] * jnp.where(far < near, 0.0, 1.0)

    for r in range(2, 18):
        c = clow[r]
        u = 4.0 * harm(c, jnp.where(top, 0.0, up(c)))
        e = 4.0 * harm(c, east(c))
        faces = [e, west(e), 4.0 * harm(c, clow[r + 1]), 4.0 * harm(c, clow[r - 1]), u, down(u)]
        diag = finish(faces, c, 64.0 * STORAGE)
        w = 0.8 * rcp(diag)
        for f in range(6):
            lcoef[f, r] = w * faces[f]
        lcoef[6, r] = w

    arrive(right_mid)
    for row in range(MID):
        joined = mid_join(mvx, 1, row)
        for k in range(2):
            mv[0, row, k] = joined[k]
            mcoef[6, row, k] = joined[k]

    def mid_sweep(p, r):
        x0, x, x2 = ([mv[p, r + d, k] for k in range(2)] for d in (-1, 0, 1))
        out = []
        for k in range(2):
            a = [mcoef[f, r, k] for f in range(7)]
            u = x[1] if k == 0 else up(x[0])
            d = x[0] if k else down(x[1])
            out.append(0.2 * x[k] + a[6] + a[0] * east(x[k]) + a[1] * west(x[k]) + a[2] * x2[k] + a[3] * x0[k]
                       + a[4] * u + a[5] * d)
        return x, out

    for j in range(1, 8):
        p, q = (j + 1) % 2, j % 2
        for r in range(j, MID - j):
            _, new = mid_sweep(p, r)
            for k in range(2):
                mv[q, r, k] = new[k]

    for i in range(4):
        acc = None
        for o in range(2):
            r = 8 + 2 * i + o
            x, new = mid_sweep(1, r)
            for k in range(2):
                res = (new[k] - x[k]) * mcoef[7, r, k]
                acc = res if acc is None else acc + res
        lvx[8 + i] = lcoef[6, 8 + i] * compact(acc, pair_low)
    right_low = low_exchange(lvx)
    start(right_low)

    for i in range(8):
        for k in range(2):
            tmid[pl.ds(k * 8 + i, 8, stride=16), :] = roll(mv[1, 8 + i, k], -MX)
    out_mid[...] = tmid[...].reshape(16, 8, 128)[:, :, :64]

    arrive(right_low)
    for j in range(1, 8):
        src, q = lvx if j == 1 else lv.at[(j + 1) % 2], j % 2
        for r in range(1 + j, LOW - 1 - j):
            x = src[r]
            a = [lcoef[f, r] for f in range(6)]
            lv[q, r] = (0.2 * x + lvx[r] + a[0] * east(x) + a[1] * west(x) + a[2] * src[r + 1] + a[3] * src[r - 1]
                        + a[4] * up(x) + a[5] * down(x))
    for i in range(4):
        tlow[pl.ds(i, 8, stride=8), :] = roll(lv[1, 8 + i], -LX)
    out_low[...] = tlow[...].reshape(8, 8, 128)[:, :4, :32]

    for c_ in cond_y + raw_x + right_y + cond_mid + cond_low + right_mid + right_low:
        c_.wait_send()


N_COPIES = 2 + 6 + 2 + 8 + 4 + 8 + 4


def per_device(ngx, ngy, permeability, source, phase_mask):
    vmem = pl.BlockSpec(memory_space=pltpu.VMEM)
    vec = lambda *dims: pltpu.VMEM(dims + (8, 128), F32)
    flat = [x.reshape(512, 128) for x in (permeability, source, phase_mask)]
    fine, mid, low = pl.pallas_call(
        functools.partial(kernel, ngx, ngy),
        out_shape=(
            jax.ShapeDtypeStruct((512, 128), F32),
            jax.ShapeDtypeStruct((16, 8, 64), F32),
            jax.ShapeDtypeStruct((8, 4, 32), F32),
        ),
        in_specs=[vmem] * 3,
        out_specs=(vmem,) * 3,
        scratch_shapes=[
            vec(ROWS, 4), vec(ROWS, 4),
            vec(16), vec(16), vec(ROWS), vec(ROWS),
            vec(ROWS), vec(ROWS), vec(ROWS),
            vec(7, ROWS, 5), vec(ROWS, 5), vec(2, ROWS, 5),
            vec(MID, 2), vec(MID, 2), vec(2, 2, 4), vec(2, 3, 4), vec(2, 3, 4),
            vec(8, MID, 2), vec(MID, 2), vec(2, MID, 2),
            vec(LOW), vec(7, LOW), vec(LOW), vec(2, LOW),
            pltpu.VMEM((128, 128), F32), pltpu.VMEM((64, 128), F32),
            pltpu.SemaphoreType.DMA((N_COPIES,)), pltpu.SemaphoreType.DMA((N_COPIES,)),
        ],
        compiler_params=pltpu.CompilerParams(
            collective_id=0, has_side_effects=True, vmem_limit_bytes=40 * 2**20),
    )(*flat)
    return fine.reshape(32, 16, 128), mid, low


def solution(mesh):
    placed = (P(None, "gy", "gx"),) * 3
    return jax.shard_map(
        functools.partial(per_device, mesh.shape["gx"], mesh.shape["gy"]),
        mesh=mesh, in_specs=placed, out_specs=placed, check_vma=False)
```

```python
import functools

import jax
import jax.numpy as jnp
from jax import lax
from jax.experimental import pallas as pl
from jax.experimental.pallas import tpu as pltpu
from jax.sharding import PartitionSpec as P

MESH = pl.DeviceIdType.MESH
F32 = jnp.float32
STORAGE = 0.05
LEAK = 0.1
TINY = 1e-30

HALO = 9
ROWS = 16 + 2 * HALO
MID = 24
LOW = 20
MX = 22
LX = 11


def rcp(d):
    r = pl.reciprocal(d, approx=True)
    return r * (2.0 - d * r)


def harm(a, b):
    return (2.0 * a * b) * rcp(jnp.maximum(a + b, TINY))


def lane_of(shape):
    return lax.broadcasted_iota(jnp.int32, shape, len(shape) - 1)


def sub_of(shape):
    return lax.broadcasted_iota(jnp.int32, shape, len(shape) - 2)


def roll(x, shift):
    shift = shift % 128
    return x if shift == 0 else pltpu.roll(x, shift, x.ndim - 1)


def east(x):
    return roll(x, 127)


def west(x):
    return roll(x, 1)


def up(x):
    return pltpu.roll(x, 7, x.ndim - 2)


def down(x):
    return pltpu.roll(x, 1, x.ndim - 2)


def strip_up(x):
    y = roll(x, 96)
    return jnp.where(lane_of(x.shape) >= 96, up(y), y)


def strip_down(x):
    y = roll(x, 32)
    return jnp.where(lane_of(x.shape) < 32, down(y), y)


def groups(parts, shifts):
    lane = lane_of(parts[0].shape)
    out = roll(parts[3], shifts[3])
    for q in (2, 1, 0):
        out = jnp.where(lane < 32 * (q + 1), roll(parts[q], shifts[q]), out)
    return out


def pack_west(m):
    return groups(m, [32 * k + 9 for k in range(4)])


def pack_east(m):
    return groups(m, [32 * k + 23 for k in range(4)])


def main_east(m, k, strip):
    ins = roll(strip, 104 - 32 * k)
    return jnp.where(lane_of(m.shape) == 127, ins, east(m))


def main_west(m, k, strip):
    ins = roll(strip, -(32 * k + 8))
    return jnp.where(lane_of(m.shape) == 0, ins, west(m))


def finish(t, c, store):
    total = t[0]
    for x in t[1:]:
        total = total + x
    return total + store * c + jnp.where(c > 0.0, 0.0, 1.0)


def kernel(ngx, ngy, perm_in, source_in, mask_in, out_fine, out_mid, out_low,
           cm, bm, own_w, own_e, own_b, sr, sl, rl, rr, cs, cse, csw, coef, inv, v,
           cmx, cmid, midx, mrl, mrr, mcoef, mvx, mv, clow, lcoef, lvx, lv, tmid, tlow, perm, source, mask, send, recv, load):
    gx, gy = lax.axis_index("gx"), lax.axis_index("gy")
    loads = [pltpu.make_async_copy(a, b, load.at[i])
             for i, (a, b) in enumerate(((perm_in, perm), (mask_in, mask), (source_in, source)))]
    for l in loads:
        l.start()

    def dev(dx, dy):
        return (lax.rem(gx + dx + ngx, ngx), lax.rem(gy + dy + 2 * ngy, ngy))

    around = [(dx, dy) for dx in (-1, 0, 1) for dy in (-1, 0, 1) if (dx, dy) != (0, 0)]
    barrier = pltpu.get_barrier_semaphore()
    for d in around:
        pl.semaphore_signal(barrier, inc=1, device_id=dev(*d), device_id_type=MESH)

    made = [0]

    def copy(src, dst, to):
        i = made[0]
        made[0] += 1
        return pltpu.make_async_remote_copy(
            src_ref=src, dst_ref=dst, send_sem=send.at[i], recv_sem=recv.at[i],
            device_id=dev(*to), device_id_type=MESH)


    def take(ref, y, k):
        return ref[pl.ds(k * 16 + y, 8, stride=64), :]

    lane = lane_of((8, 128))
    c32 = jnp.bitwise_and(lane, 31)
    sub = sub_of((8, 128))
    pair_mid = jnp.clip(2 * (lane - MX), 0, 127)
    pair_low = jnp.clip(2 * lane, 0, 127)

    def compact(x, index):
        return jnp.take_along_axis(x + east(x), index, axis=1, mode="promise_in_bounds")

    for l in loads:
        l.wait()

    def load_pair(i, carry):
        acc = [None, None]
        for o in range(2):
            y = 2 * i + o
            conds, rights = [], []
            for k in range(4):
                p, m = take(perm, y, k), take(mask, y, k)
                c = jnp.where(m == 2, 0.0, p)
                b = jnp.where(m == 1, take(source, y, k), 0.0)
                cm[HALO + y, k] = c
                bm[HALO + y, k] = b
                conds.append(c)
                rights.append(b)
                term = LEAK * p + (1.0 - LEAK) * c
                acc[k // 2] = term if acc[k // 2] is None else acc[k // 2] + term
            aw, ae = pack_west(conds), pack_east(conds)
            bw, be = pack_west(rights), pack_east(rights)
            own_w[y], own_e[y] = aw, ae
            own_b[y] = jnp.where(c32 < 16, bw, be)
            sr[y] = jnp.where(c32 < 16, aw, roll(bw, 16))
            sl[y] = jnp.where(c32 >= 16, ae, roll(be, 112))
        for k in range(2):
            cmx[8 + i, k] = compact(acc[k], pair_mid) * 0.125
        return carry

    lax.fori_loop(0, 8, load_pair, 0, unroll=True)

    def mid_pack(src, row0, slot):
        for i in range(4):
            parts = [src[row0 + i + 4 * (q // 2), q % 2] for q in range(4)]
            midx[slot, 0, i] = groups(parts, [32 * q - (MX + 42) for q in range(4)])
            midx[slot, 1, i] = groups(parts, [32 * q - MX for q in range(4)])

    mid_pack(cmx, 8, 0)
    pl.semaphore_wait(barrier, len(around))

    def start(cs_):
        for c_ in cs_:
            c_.start()

    def arrive(cs_):
        for c_ in cs_:
            c_.wait_recv()

    def strips(src_r, src_l, dst_l, dst_r, n):
        own = src_r.shape[0]
        got = []
        for dx, src, dst in ((1, src_r, dst_l), (-1, src_l, dst_r)):
            got.append(copy(src, dst.at[pl.ds(n, own)], (dx, 0)))
            got.append(copy(src.at[pl.ds(own - n, n)], dst.at[pl.ds(0, n)], (dx, 1)))
            got.append(copy(src.at[pl.ds(0, n)], dst.at[pl.ds(n + own, n)], (dx, -1)))
        return got

    def edges(buf, n, own, first=0):
        return [copy(buf.at[pl.ds(first + own, n)], buf.at[pl.ds(first, n)], (0, 1)),
                copy(buf.at[pl.ds(first + n, n)], buf.at[pl.ds(first + n + own, n)], (0, -1))]

    cond_y = edges(cm, HALO, 16)
    raw_x = strips(sr, sl, rl, rr, HALO)
    right_y = edges(bm, HALO, 16)
    start(cond_y + raw_x + right_y)

    def mid_exchange(buf, slot):
        got = edges(buf, 8, 8)
        for dx, side, dst in ((1, 0, mrl), (-1, 1, mrr)):
            src = midx.at[slot, side]
            for dy, block in ((0, 1), (1, 0), (-1, 2)):
                got.append(copy(src, dst.at[slot, block], (dx, dy)))
        return got

    cond_mid = mid_exchange(cmx, 0)
    start(cond_mid)

    inside = jnp.where(gx == 0, 9, 0), jnp.where(gx == ngx - 1, 23, 32)
    keep = (c32 >= inside[0]) & (c32 < inside[1])

    def strip_cond(r, aw, ae, live=None):
        c = jnp.where(c32 < 9, rl[r], jnp.where(c32 < 16, aw, jnp.where(c32 < 23, ae, rr[r])))
        c = jnp.where(keep, c, 0.0)
        if live is not None:
            c = c * live
        cs[r] = c
        cse[r] = east(jnp.where(c32 == 16, aw, c))
        csw[r] = west(jnp.where(c32 == 15, ae, c))

    top = sub == 7

    def fine_coefs(r):
        m = [[cm[r + d, k] for k in range(4)] for d in (-1, 0, 1)]
        s = [cs[r + d] for d in (-1, 0, 1)]
        se = cse[r]
        c = s[1]
        te = harm(c, se)
        tw = harm(c, csw[r])
        tn, ts = harm(c, s[2]), harm(c, s[0])
        tu = harm(c, jnp.where(top & (lane >= 96), 0.0, strip_up(c)))
        faces = [te, tw, tn, ts, tu, strip_down(tu)]

        def put(k, faces, c):
            diag = finish(faces, c, STORAGE)
            w = 0.8 * rcp(diag)
            for f in range(6):
                coef[f, r, k] = w * faces[f]
            coef[6, r, k] = w
            inv[r, k] = 1.25 * diag

        put(4, faces, c)
        ups = [harm(m[1][k], m[1][k + 1]) for k in range(3)]
        ups.append(harm(m[1][3], jnp.where(top, 0.0, up(m[1][0]))))
        for k in range(4):
            c = m[1][k]
            e = harm(c, main_east(c, k, s[1]))
            w_ = main_west(e, k, te)
            d_ = ups[k - 1] if k else down(ups[3])
            put(k, [e, w_, harm(c, m[2][k]), harm(c, m[0][k]), ups[k], d_], c)

    def first(r, mid):
        b = [bm[r, k] for k in range(4)]
        b.append(jnp.where(c32 < 9, roll(rl[r], 112), jnp.where(c32 < 23, mid, roll(rr[r], 16))))
        for k in range(5):
            x = coef[6, r, k] * b[k]
            v[r, k] = x
            coef[6, r, k] = x

    def loop(n, unroll):
        def run(body):
            def step(i, carry):
                body(i)
                return carry
            lax.fori_loop(0, n, step, 0, unroll=unroll)
        return run

    arrive([raw_x[0], raw_x[3]])

    @loop(16, True)
    def _(i):
        strip_cond(HALO + i, own_w[i], own_e[i])

    @loop(14, 7)
    def _(i):
        fine_coefs(HALO + 1 + i)

    @loop(14, 7)
    def _(i):
        first(HALO + 1 + i, own_b[1 + i])

    arrive(cond_y + raw_x[1:3] + raw_x[4:6])

    @pl.when(gy == 0)
    def _():
        cm[pl.ds(0, HALO)] = jnp.zeros((HALO, 4, 8, 128), F32)

    @pl.when(gy == ngy - 1)
    def _():
        cm[pl.ds(16 + HALO, HALO)] = jnp.zeros((HALO, 4, 8, 128), F32)

    lives = [jnp.where(gy == 0, 0.0, 1.0), jnp.where(gy == ngy - 1, 0.0, 1.0)]

    @loop(HALO, True)
    def _(i):
        for r, live in ((i, lives[0]), (16 + HALO + i, lives[1])):
            parts = [cm[r, k] for k in range(4)]
            strip_cond(r, pack_west(parts), pack_east(parts), live)

    @loop(HALO, 3)
    def _(i):
        for r in (1 + i, 15 + HALO + i):
            fine_coefs(r)

    arrive(right_y)
    first(HALO, own_b[0])
    first(HALO + 15, own_b[15])

    @loop(HALO - 1, 4)
    def _(i):
        for r in (1 + i, 16 + HALO + i):
            parts = [bm[r, k] for k in range(4)]
            first(r, jnp.where(c32 < 16, pack_west(parts), pack_east(parts)))

    def sweep_main(r, k, x, x0, x2, strip):
        u = x[k + 1] if k < 3 else up(x[0])
        d = x[k - 1] if k else down(x[3])
        a = [coef[f, r, k] for f in range(7)]
        return (0.2 * x[k] + a[6] + a[0] * main_east(x[k], k, strip) + a[1] * main_west(x[k], k, strip)
                + a[2] * x2[k] + a[3] * x0[k] + a[4] * u + a[5] * d)

    def row_in(r):
        return [v[r, k] for k in range(5)]

    def sweep_row(r, x0, x, x2):
        s = x[4]
        for k in range(4):
            v[r, k] = sweep_main(r, k, x, x0, x2, s)
        a = [coef[f, r, 4] for f in range(7)]
        v[r, 4] = (0.2 * s + a[6] + a[0] * east(s) + a[1] * west(s) + a[2] * x2[4] + a[3] * x0[4]
                   + a[4] * strip_up(s) + a[5] * strip_down(s))

    def sweep_rows(r0, n, x0, x):
        for o in range(n):
            x2 = row_in(r0 + o + 1)
            sweep_row(r0 + o, x0, x, x2)
            x0, x = x, x2
        return x0, x

    for j in range(1, 8):
        sweep_rows(j + 1, ROWS - 2 - 2 * j, row_in(j), row_in(j + 1))

    def mid_join(buf, slot, row):
        block, i = row // 8, row % 8
        out = []
        for k in range(2):
            q = 2 * (i // 4) + k
            left = roll(mrl[slot, block, i % 4], -32 * q)
            right = roll(mrr[slot, block, i % 4], MX + 64 - 32 * q)
            out.append(jnp.where(lane < MX, left, jnp.where(lane < MX + 64, buf[row, k], right)))
        return out

    arrive(cond_mid)
    lo, hi = jnp.where(gx == 0, MX, 0), jnp.where(gx == ngx - 1, MX + 64, 128)
    keep_mid = (lane >= lo) & (lane < hi)

    def join_cond(row):
        joined = mid_join(cmx, 0, row)
        for k in range(2):
            c = jnp.where(keep_mid, joined[k], 0.0)
            cmid[row, k] = c if row // 8 == 1 else c * lives[row // 16]

    def mid_coefs(r):
        x = [[cmid[r + d, k] for k in range(2)] for d in (-1, 0, 1)]
        u = [2.0 * harm(x[1][0], x[1][1]), 2.0 * harm(x[1][1], jnp.where(top, 0.0, up(x[1][0])))]
        for k in range(2):
            c = x[1][k]
            e = 2.0 * harm(c, east(c))
            faces = [e, west(e), 2.0 * harm(c, x[2][k]), 2.0 * harm(c, x[0][k]), u[k], u[0] if k else down(u[1])]
            diag = finish(faces, c, 8.0 * STORAGE)
            w = 0.8 * rcp(diag)
            for f in range(6):
                mcoef[f, r, k] = w * faces[f]
            mcoef[6, r, k] = w
            mcoef[7, r, k] = 1.25 * diag

    for row in range(7, 17):
        join_cond(row)
    for row in range(8, 16):
        mid_coefs(row)

    for i in range(4):
        acc = cmid[8 + 2 * i, 0] + cmid[8 + 2 * i, 1] + cmid[9 + 2 * i, 0] + cmid[9 + 2 * i, 1]
        clow[8 + i] = compact(acc, pair_low) * 0.125

    def low_exchange(buf):
        return [copy(buf.at[pl.ds(8, 4)], buf.at[pl.ds(4, 4)], (0, 1)),
                copy(buf.at[pl.ds(8, 4)], buf.at[pl.ds(12, 4)], (0, -1)),
                copy(buf.at[pl.ds(8, 4)], buf.at[pl.ds(0, 4)], (0, 2)),
                copy(buf.at[pl.ds(8, 4)], buf.at[pl.ds(16, 4)], (0, -2))]

    cond_low = low_exchange(clow)
    start(cond_low)

    def fine_residual(i, carry):
        acc = [None, None]
        r0 = HALO + 2 * i
        rows = [[v[r0 + o - 1, k] for k in range(4)] for o in range(4)]
        for o in range(2):
            r = r0 + o
            x0, x, x2 = rows[o], rows[o + 1], rows[o + 2]
            strip = v[r, 4]
            for k in range(4):
                res = (sweep_main(r, k, x, x0, x2, strip) - x[k]) * inv[r, k]
                acc[k // 2] = res if acc[k // 2] is None else acc[k // 2] + res
        for k in range(2):
            mvx[8 + i, k] = mcoef[6, 8 + i, k] * compact(acc[k], pair_mid)
        return carry

    lax.fori_loop(0, 8, fine_residual, 0, unroll=4)
    mid_pack(mvx, 8, 1)
    right_mid = mid_exchange(mvx, 1)
    start(right_mid)

    for row in list(range(7)) + list(range(17, MID)):
        join_cond(row)
    for row in list(range(1, 8)) + list(range(16, MID - 1)):
        mid_coefs(row)

    def write_fine(y, carry):
        for k in range(4):
            out_fine[pl.ds(k * 16 + y, 8, stride=64), :] = v[HALO + y, k]
        return carry

    lax.fori_loop(0, 16, write_fine, 0, unroll=True)

    arrive(cond_low)
    for row in list(range(1, 8)) + list(range(12, 19)):
        far = ngy - 1 - gy if row >= 12 else gy
        near = (row - 12) // 4 + 1 if row >= 12 else (11 - row) // 4
        clow[row] = clow[row] * jnp.where(far < near, 0.0, 1.0)

    for r in range(2, 18):
        c = clow[r]
        u = 4.0 * harm(c, jnp.where(top, 0.0, up(c)))
        e = 4.0 * harm(c, east(c))
        faces = [e, west(e), 4.0 * harm(c, clow[r + 1]), 4.0 * harm(c, clow[r - 1]), u, down(u)]
        diag = finish(faces, c, 64.0 * STORAGE)
        w = 0.8 * rcp(diag)
        for f in range(6):
            lcoef[f, r] = w * faces[f]
        lcoef[6, r] = w

    arrive(right_mid)
    for row in range(MID):
        joined = mid_join(mvx, 1, row)
        for k in range(2):
            mv[0, row, k] = joined[k]
            mcoef[6, row, k] = joined[k]

    def mid_sweep(p, r):
        x0, x, x2 = ([mv[p, r + d, k] for k in range(2)] for d in (-1, 0, 1))
        out = []
        for k in range(2):
            a = [mcoef[f, r, k] for f in range(7)]
            u = x[1] if k == 0 else up(x[0])
            d = x[0] if k else down(x[1])
            out.append(0.2 * x[k] + a[6] + a[0] * east(x[k]) + a[1] * west(x[k]) + a[2] * x2[k] + a[3] * x0[k]
                       + a[4] * u + a[5] * d)
        return x, out

    for j in range(1, 8):
        p, q = (j + 1) % 2, j % 2
        for r in range(j, MID - j):
            _, new = mid_sweep(p, r)
            for k in range(2):
                mv[q, r, k] = new[k]

    for i in range(4):
        acc = None
        for o in range(2):
            r = 8 + 2 * i + o
            x, new = mid_sweep(1, r)
            for k in range(2):
                res = (new[k] - x[k]) * mcoef[7, r, k]
                acc = res if acc is None else acc + res
        lvx[8 + i] = lcoef[6, 8 + i] * compact(acc, pair_low)
    right_low = low_exchange(lvx)
    start(right_low)

    for i in range(8):
        for k in range(2):
            tmid[pl.ds(k * 8 + i, 8, stride=16), :] = roll(mv[1, 8 + i, k], -MX)
    out_mid[...] = tmid[...].reshape(16, 8, 128)[:, :, :64]

    arrive(right_low)
    for j in range(1, 8):
        src, q = lvx if j == 1 else lv.at[(j + 1) % 2], j % 2
        for r in range(1 + j, LOW - 1 - j):
            x = src[r]
            a = [lcoef[f, r] for f in range(6)]
            lv[q, r] = (0.2 * x + lvx[r] + a[0] * east(x) + a[1] * west(x) + a[2] * src[r + 1] + a[3] * src[r - 1]
                        + a[4] * up(x) + a[5] * down(x))
    for i in range(4):
        tlow[pl.ds(i, 8, stride=8), :] = roll(lv[1, 8 + i], -LX)
    out_low[...] = tlow[...].reshape(8, 8, 128)[:, :4, :32]

    for c_ in cond_y + raw_x + right_y + cond_mid + cond_low + right_mid + right_low:
        c_.wait_send()


N_COPIES = 2 + 6 + 2 + 8 + 4 + 8 + 4


def per_device(ngx, ngy, permeability, source, phase_mask):
    vmem = pl.BlockSpec(memory_space=pltpu.VMEM)
    vec = lambda *dims: pltpu.VMEM(dims + (8, 128), F32)
    flat = [x.reshape(512, 128) for x in (permeability, source, phase_mask)]
    fine, mid, low = pl.pallas_call(
        functools.partial(kernel, ngx, ngy),
        out_shape=(
            jax.ShapeDtypeStruct((512, 128), F32),
            jax.ShapeDtypeStruct((16, 8, 64), F32),
            jax.ShapeDtypeStruct((8, 4, 32), F32),
        ),
        in_specs=[pl.BlockSpec(memory_space=pl.ANY)] * 3,
        out_specs=(vmem,) * 3,
        scratch_shapes=[
            vec(ROWS, 4), vec(ROWS, 4),
            vec(16), vec(16), vec(16),
            vec(16), vec(16), vec(ROWS), vec(ROWS),
            vec(ROWS), vec(ROWS), vec(ROWS),
            vec(7, ROWS, 5), vec(ROWS, 5), vec(ROWS, 5),
            vec(MID, 2), vec(MID, 2), vec(2, 2, 4), vec(2, 3, 4), vec(2, 3, 4),
            vec(8, MID, 2), vec(MID, 2), vec(2, MID, 2),
            vec(LOW), vec(7, LOW), vec(LOW), vec(2, LOW),
            pltpu.VMEM((128, 128), F32), pltpu.VMEM((64, 128), F32),
            pltpu.VMEM((512, 128), F32), pltpu.VMEM((512, 128), F32), pltpu.VMEM((512, 128), jnp.int32),
            pltpu.SemaphoreType.DMA((N_COPIES,)), pltpu.SemaphoreType.DMA((N_COPIES,)),
            pltpu.SemaphoreType.DMA((3,)),
        ],
        compiler_params=pltpu.CompilerParams(
            collective_id=0, has_side_effects=True, vmem_limit_bytes=40 * 2**20),
    )(*flat)
    return fine.reshape(32, 16, 128), mid, low


def solution(mesh):
    placed = (P(None, "gy", "gx"),) * 3
    return jax.shard_map(
        functools.partial(per_device, mesh.shape["gx"], mesh.shape["gy"]),
        mesh=mesh, in_specs=placed, out_specs=placed, check_vma=False)
```

```python
import functools

import jax
import jax.numpy as jnp
from jax import lax
from jax.experimental import pallas as pl
from jax.experimental.pallas import tpu as pltpu
from jax.sharding import PartitionSpec as P

MESH = pl.DeviceIdType.MESH
F32 = jnp.float32
STORAGE = 0.05
LEAK = 0.1
TINY = 1e-30

HALO = 9
ROWS = 16 + 2 * HALO
MID = 24
LOW = 20
MX = 22
LX = 11


def rcp(d):
    r = pl.reciprocal(d, approx=True)
    return r * (2.0 - d * r)


def harm(a, b):
    return (2.0 * a * b) * rcp(jnp.maximum(a + b, TINY))


def lane_of(shape):
    return lax.broadcasted_iota(jnp.int32, shape, len(shape) - 1)


def sub_of(shape):
    return lax.broadcasted_iota(jnp.int32, shape, len(shape) - 2)


def roll(x, shift):
    shift = shift % 128
    return x if shift == 0 else pltpu.roll(x, shift, x.ndim - 1)


def east(x):
    return roll(x, 127)


def west(x):
    return roll(x, 1)


def up(x):
    return pltpu.roll(x, 7, x.ndim - 2)


def down(x):
    return pltpu.roll(x, 1, x.ndim - 2)


def strip_up(x):
    y = roll(x, 96)
    return jnp.where(lane_of(x.shape) >= 96, up(y), y)


def strip_down(x):
    y = roll(x, 32)
    return jnp.where(lane_of(x.shape) < 32, down(y), y)


def groups(parts, shifts):
    lane = lane_of(parts[0].shape)
    out = roll(parts[3], shifts[3])
    for q in (2, 1, 0):
        out = jnp.where(lane < 32 * (q + 1), roll(parts[q], shifts[q]), out)
    return out


def pack_west(m):
    return groups(m, [32 * k + 9 for k in range(4)])


def pack_east(m):
    return groups(m, [32 * k + 23 for k in range(4)])


def main_east(m, k, strip):
    ins = roll(strip, 104 - 32 * k)
    return jnp.where(lane_of(m.shape) == 127, ins, east(m))


def main_west(m, k, strip):
    ins = roll(strip, -(32 * k + 8))
    return jnp.where(lane_of(m.shape) == 0, ins, west(m))


def finish(t, c, store):
    total = t[0]
    for x in t[1:]:
        total = total + x
    return total + store * c + jnp.where(c > 0.0, 0.0, 1.0)


def kernel(ngx, ngy, perm_in, source_in, mask_in, out_fine, out_mid, out_low,
           cm, bm, own_w, own_e, own_b, sr, sl, rl, rr, cs, cse, csw, coef, inv, v,
           cmx, cmid, midx, mrl, mrr, mcoef, mvx, mv, clow, lcoef, lvx, lv, tmid, tlow, perm, source, mask, send, recv, load):
    gx, gy = lax.axis_index("gx"), lax.axis_index("gy")
    loads = [pltpu.make_async_copy(a, b, load.at[i])
             for i, (a, b) in enumerate(((perm_in, perm), (mask_in, mask), (source_in, source)))]
    for l in loads:
        l.start()

    def dev(dx, dy):
        return (lax.rem(gx + dx + ngx, ngx), lax.rem(gy + dy + 2 * ngy, ngy))

    around = [(dx, dy) for dx in (-1, 0, 1) for dy in (-1, 0, 1) if (dx, dy) != (0, 0)]
    barrier = pltpu.get_barrier_semaphore()
    for d in around:
        pl.semaphore_signal(barrier, inc=1, device_id=dev(*d), device_id_type=MESH)

    made = [0]

    def copy(src, dst, to):
        i = made[0]
        made[0] += 1
        return pltpu.make_async_remote_copy(
            src_ref=src, dst_ref=dst, send_sem=send.at[i], recv_sem=recv.at[i],
            device_id=dev(*to), device_id_type=MESH)


    def take(ref, y, k):
        return ref[pl.ds(k * 16 + y, 8, stride=64), :]

    lane = lane_of((8, 128))
    c32 = jnp.bitwise_and(lane, 31)
    sub = sub_of((8, 128))
    pair_mid = jnp.clip(2 * (lane - MX), 0, 127)
    pair_low = jnp.clip(2 * lane, 0, 127)

    def compact(x, index):
        return jnp.take_along_axis(x + east(x), index, axis=1, mode="promise_in_bounds")

    for l in loads:
        l.wait()

    def load_pair(i, carry):
        for o in range(2):
            y = 2 * i + o
            conds, rights = [], []
            for k in range(4):
                m = take(mask, y, k)
                c = jnp.where(m == 2, 0.0, take(perm, y, k))
                b = jnp.where(m == 1, take(source, y, k), 0.0)
                cm[HALO + y, k] = c
                bm[HALO + y, k] = b
                conds.append(c)
                rights.append(b)
            aw, ae = pack_west(conds), pack_east(conds)
            bw, be = pack_west(rights), pack_east(rights)
            own_w[y], own_e[y] = aw, ae
            own_b[y] = jnp.where(c32 < 16, bw, be)
            sr[y] = jnp.where(c32 < 16, aw, roll(bw, 16))
            sl[y] = jnp.where(c32 >= 16, ae, roll(be, 112))
        return carry

    def cond_pair(i, carry):
        acc = [None, None]
        for y in (2 * i, 2 * i + 1):
            for k in range(4):
                term = LEAK * take(perm, y, k) + (1.0 - LEAK) * cm[HALO + y, k]
                acc[k // 2] = term if acc[k // 2] is None else acc[k // 2] + term
        for k in range(2):
            cmx[8 + i, k] = compact(acc[k], pair_mid) * 0.125
        return carry

    lax.fori_loop(0, 8, load_pair, 0, unroll=True)

    def mid_pack(src, row0, slot):
        for i in range(4):
            parts = [src[row0 + i + 4 * (q // 2), q % 2] for q in range(4)]
            midx[slot, 0, i] = groups(parts, [32 * q - (MX + 42) for q in range(4)])
            midx[slot, 1, i] = groups(parts, [32 * q - MX for q in range(4)])

    pl.semaphore_wait(barrier, len(around))

    def start(cs_):
        for c_ in cs_:
            c_.start()

    def arrive(cs_):
        for c_ in cs_:
            c_.wait_recv()

    def strips(src_r, src_l, dst_l, dst_r, n):
        own = src_r.shape[0]
        got = []
        for dx, src, dst in ((1, src_r, dst_l), (-1, src_l, dst_r)):
            got.append(copy(src, dst.at[pl.ds(n, own)], (dx, 0)))
            got.append(copy(src.at[pl.ds(own - n, n)], dst.at[pl.ds(0, n)], (dx, 1)))
            got.append(copy(src.at[pl.ds(0, n)], dst.at[pl.ds(n + own, n)], (dx, -1)))
        return got

    def edges(buf, n, own, halo):
        return [copy(buf.at[pl.ds(halo + own - n, n)], buf.at[pl.ds(halo - n, n)], (0, 1)),
                copy(buf.at[pl.ds(halo, n)], buf.at[pl.ds(halo + own, n)], (0, -1))]

    cond_y = edges(cm, HALO, 16, HALO)
    raw_x = strips(sr, sl, rl, rr, HALO)
    right_y = edges(bm, HALO - 1, 16, HALO)
    start(cond_y + raw_x)

    def mid_exchange(buf, slot):
        got = []
        for block, dy in ((0, 1), (2, -1), (1, 0)):
            for dx, side, dst in ((1, 0, mrl), (-1, 1, mrr)):
                got.append(copy(midx.at[slot, side], dst.at[slot, block], (dx, dy)))
        return got[:4] + edges(buf, 8, 8, 8) + got[4:]

    lax.fori_loop(0, 8, cond_pair, 0, unroll=4)
    mid_pack(cmx, 8, 0)
    cond_mid = mid_exchange(cmx, 0)
    start(cond_mid + right_y)

    inside = jnp.where(gx == 0, 9, 0), jnp.where(gx == ngx - 1, 23, 32)
    keep = (c32 >= inside[0]) & (c32 < inside[1])

    def strip_cond(r, aw, ae, live=None):
        c = jnp.where(c32 < 9, rl[r], jnp.where(c32 < 16, aw, jnp.where(c32 < 23, ae, rr[r])))
        c = jnp.where(keep, c, 0.0)
        if live is not None:
            c = c * live
        cs[r] = c
        cse[r] = east(jnp.where(c32 == 16, aw, c))
        csw[r] = west(jnp.where(c32 == 15, ae, c))

    top = sub == 7

    def fine_coefs(r):
        m = [[cm[r + d, k] for k in range(4)] for d in (-1, 0, 1)]
        s = [cs[r + d] for d in (-1, 0, 1)]
        se = cse[r]
        c = s[1]
        te = harm(c, se)
        tw = harm(c, csw[r])
        tn, ts = harm(c, s[2]), harm(c, s[0])
        tu = harm(c, jnp.where(top & (lane >= 96), 0.0, strip_up(c)))
        faces = [te, tw, tn, ts, tu, strip_down(tu)]

        def put(k, faces, c):
            diag = finish(faces, c, STORAGE)
            w = 0.8 * rcp(diag)
            for f in range(6):
                coef[f, r, k] = w * faces[f]
            coef[6, r, k] = w
            inv[r, k] = 1.25 * diag

        put(4, faces, c)
        ups = [harm(m[1][k], m[1][k + 1]) for k in range(3)]
        ups.append(harm(m[1][3], jnp.where(top, 0.0, up(m[1][0]))))
        for k in range(4):
            c = m[1][k]
            e = harm(c, main_east(c, k, s[1]))
            w_ = main_west(e, k, te)
            d_ = ups[k - 1] if k else down(ups[3])
            put(k, [e, w_, harm(c, m[2][k]), harm(c, m[0][k]), ups[k], d_], c)

    def first(r, mid):
        b = [bm[r, k] for k in range(4)]
        b.append(jnp.where(c32 < 9, roll(rl[r], 112), jnp.where(c32 < 23, mid, roll(rr[r], 16))))
        for k in range(5):
            x = coef[6, r, k] * b[k]
            v[r, k] = x
            coef[6, r, k] = x

    def loop(n, unroll):
        def run(body):
            def step(i, carry):
                body(i)
                return carry
            lax.fori_loop(0, n, step, 0, unroll=unroll)
        return run

    arrive([raw_x[0], raw_x[3]])

    @loop(16, True)
    def _(i):
        strip_cond(HALO + i, own_w[i], own_e[i])

    @loop(14, 7)
    def _(i):
        fine_coefs(HALO + 1 + i)

    @loop(14, 7)
    def _(i):
        first(HALO + 1 + i, own_b[1 + i])

    arrive(cond_y + raw_x[1:3] + raw_x[4:6])

    @pl.when(gy == 0)
    def _():
        cm[pl.ds(0, HALO)] = jnp.zeros((HALO, 4, 8, 128), F32)

    @pl.when(gy == ngy - 1)
    def _():
        cm[pl.ds(16 + HALO, HALO)] = jnp.zeros((HALO, 4, 8, 128), F32)

    lives = [jnp.where(gy == 0, 0.0, 1.0), jnp.where(gy == ngy - 1, 0.0, 1.0)]

    @loop(HALO, True)
    def _(i):
        for r, live in ((i, lives[0]), (16 + HALO + i, lives[1])):
            parts = [cm[r, k] for k in range(4)]
            strip_cond(r, pack_west(parts), pack_east(parts), live)

    @loop(HALO, 3)
    def _(i):
        for r in (1 + i, 15 + HALO + i):
            fine_coefs(r)

    def mid_join(buf, slot, row):
        block, i = row // 8, row % 8
        out = []
        for k in range(2):
            q = 2 * (i // 4) + k
            left = roll(mrl[slot, block, i % 4], -32 * q)
            right = roll(mrr[slot, block, i % 4], MX + 64 - 32 * q)
            out.append(jnp.where(lane < MX, left, jnp.where(lane < MX + 64, buf[row, k], right)))
        return out

    arrive(cond_mid)
    lo, hi = jnp.where(gx == 0, MX, 0), jnp.where(gx == ngx - 1, MX + 64, 128)
    keep_mid = (lane >= lo) & (lane < hi)

    def join_cond(row):
        joined = mid_join(cmx, 0, row)
        for k in range(2):
            c = jnp.where(keep_mid, joined[k], 0.0)
            cmid[row, k] = c if row // 8 == 1 else c * lives[row // 16]

    def mid_coefs(r):
        x = [[cmid[r + d, k] for k in range(2)] for d in (-1, 0, 1)]
        u = [2.0 * harm(x[1][0], x[1][1]), 2.0 * harm(x[1][1], jnp.where(top, 0.0, up(x[1][0])))]
        for k in range(2):
            c = x[1][k]
            e = 2.0 * harm(c, east(c))
            faces = [e, west(e), 2.0 * harm(c, x[2][k]), 2.0 * harm(c, x[0][k]), u[k], u[0] if k else down(u[1])]
            diag = finish(faces, c, 8.0 * STORAGE)
            w = 0.8 * rcp(diag)
            for f in range(6):
                mcoef[f, r, k] = w * faces[f]
            mcoef[6, r, k] = w
            mcoef[7, r, k] = 1.25 * diag

    for row in range(7, 17):
        join_cond(row)
    for row in range(8, 16):
        mid_coefs(row)

    for i in range(4):
        acc = cmid[8 + 2 * i, 0] + cmid[8 + 2 * i, 1] + cmid[9 + 2 * i, 0] + cmid[9 + 2 * i, 1]
        clow[8 + i] = compact(acc, pair_low) * 0.125

    def low_exchange(buf):
        return [copy(buf.at[pl.ds(8, 4)], buf.at[pl.ds(4, 4)], (0, 1)),
                copy(buf.at[pl.ds(8, 4)], buf.at[pl.ds(12, 4)], (0, -1)),
                copy(buf.at[pl.ds(8, 4)], buf.at[pl.ds(0, 4)], (0, 2)),
                copy(buf.at[pl.ds(8, 4)], buf.at[pl.ds(16, 4)], (0, -2))]

    cond_low = low_exchange(clow)
    start(cond_low)

    arrive(right_y)
    first(HALO, own_b[0])
    first(HALO + 15, own_b[15])

    @loop(HALO - 1, 4)
    def _(i):
        for r in (1 + i, 16 + HALO + i):
            parts = [bm[r, k] for k in range(4)]
            first(r, jnp.where(c32 < 16, pack_west(parts), pack_east(parts)))

    def sweep_main(r, k, x, x0, x2, strip):
        u = x[k + 1] if k < 3 else up(x[0])
        d = x[k - 1] if k else down(x[3])
        a = [coef[f, r, k] for f in range(7)]
        return (0.2 * x[k] + a[6] + a[0] * main_east(x[k], k, strip) + a[1] * main_west(x[k], k, strip)
                + a[2] * x2[k] + a[3] * x0[k] + a[4] * u + a[5] * d)

    def row_in(r):
        return [v[r, k] for k in range(5)]

    def sweep_row(r, x0, x, x2):
        s = x[4]
        for k in range(4):
            v[r, k] = sweep_main(r, k, x, x0, x2, s)
        a = [coef[f, r, 4] for f in range(7)]
        v[r, 4] = (0.2 * s + a[6] + a[0] * east(s) + a[1] * west(s) + a[2] * x2[4] + a[3] * x0[4]
                   + a[4] * strip_up(s) + a[5] * strip_down(s))

    def sweep_rows(r0, n, x0, x):
        for o in range(n):
            x2 = row_in(r0 + o + 1)
            sweep_row(r0 + o, x0, x, x2)
            x0, x = x, x2
        return x0, x

    for j in range(1, 8):
        sweep_rows(j + 1, ROWS - 2 - 2 * j, row_in(j), row_in(j + 1))

    def fine_residual(i, carry):
        acc = [None, None]
        r0 = HALO + 2 * i
        rows = [[v[r0 + o - 1, k] for k in range(4)] for o in range(4)]
        for o in range(2):
            r = r0 + o
            x0, x, x2 = rows[o], rows[o + 1], rows[o + 2]
            strip = v[r, 4]
            for k in range(4):
                res = (sweep_main(r, k, x, x0, x2, strip) - x[k]) * inv[r, k]
                acc[k // 2] = res if acc[k // 2] is None else acc[k // 2] + res
        for k in range(2):
            mvx[8 + i, k] = mcoef[6, 8 + i, k] * compact(acc[k], pair_mid)
        return carry

    lax.fori_loop(0, 8, fine_residual, 0, unroll=4)
    mid_pack(mvx, 8, 1)
    right_mid = mid_exchange(mvx, 1)
    start(right_mid)

    for row in list(range(7)) + list(range(17, MID)):
        join_cond(row)
    for row in list(range(1, 8)) + list(range(16, MID - 1)):
        mid_coefs(row)

    def write_fine(y, carry):
        for k in range(4):
            out_fine[pl.ds(k * 16 + y, 8, stride=64), :] = v[HALO + y, k]
        return carry

    lax.fori_loop(0, 16, write_fine, 0, unroll=True)

    arrive(cond_low)
    for row in list(range(1, 8)) + list(range(12, 19)):
        far = ngy - 1 - gy if row >= 12 else gy
        near = (row - 12) // 4 + 1 if row >= 12 else (11 - row) // 4
        clow[row] = clow[row] * jnp.where(far < near, 0.0, 1.0)

    for r in range(2, 18):
        c = clow[r]
        u = 4.0 * harm(c, jnp.where(top, 0.0, up(c)))
        e = 4.0 * harm(c, east(c))
        faces = [e, west(e), 4.0 * harm(c, clow[r + 1]), 4.0 * harm(c, clow[r - 1]), u, down(u)]
        diag = finish(faces, c, 64.0 * STORAGE)
        w = 0.8 * rcp(diag)
        for f in range(6):
            lcoef[f, r] = w * faces[f]
        lcoef[6, r] = w

    arrive(right_mid)
    for row in range(MID):
        joined = mid_join(mvx, 1, row)
        for k in range(2):
            mv[0, row, k] = joined[k]
            mcoef[6, row, k] = joined[k]

    def mid_sweep(p, r):
        x0, x, x2 = ([mv[p, r + d, k] for k in range(2)] for d in (-1, 0, 1))
        out = []
        for k in range(2):
            a = [mcoef[f, r, k] for f in range(7)]
            u = x[1] if k == 0 else up(x[0])
            d = x[0] if k else down(x[1])
            out.append(0.2 * x[k] + a[6] + a[0] * east(x[k]) + a[1] * west(x[k]) + a[2] * x2[k] + a[3] * x0[k]
                       + a[4] * u + a[5] * d)
        return x, out

    for j in range(1, 8):
        p, q = (j + 1) % 2, j % 2
        for r in range(j, MID - j):
            _, new = mid_sweep(p, r)
            for k in range(2):
                mv[q, r, k] = new[k]

    for i in range(4):
        acc = None
        for o in range(2):
            r = 8 + 2 * i + o
            x, new = mid_sweep(1, r)
            for k in range(2):
                res = (new[k] - x[k]) * mcoef[7, r, k]
                acc = res if acc is None else acc + res
        lvx[8 + i] = lcoef[6, 8 + i] * compact(acc, pair_low)
    right_low = low_exchange(lvx)
    start(right_low)

    for i in range(8):
        for k in range(2):
            tmid[pl.ds(k * 8 + i, 8, stride=16), :] = roll(mv[1, 8 + i, k], -MX)
    out_mid[...] = tmid[...].reshape(16, 8, 128)[:, :, :64]

    arrive(right_low)
    for j in range(1, 8):
        src, q = lvx if j == 1 else lv.at[(j + 1) % 2], j % 2
        for r in range(1 + j, LOW - 1 - j):
            x = src[r]
            a = [lcoef[f, r] for f in range(6)]
            lv[q, r] = (0.2 * x + lvx[r] + a[0] * east(x) + a[1] * west(x) + a[2] * src[r + 1] + a[3] * src[r - 1]
                        + a[4] * up(x) + a[5] * down(x))
    for i in range(4):
        tlow[pl.ds(i, 8, stride=8), :] = roll(lv[1, 8 + i], -LX)
    out_low[...] = tlow[...].reshape(8, 8, 128)[:, :4, :32]

    for c_ in cond_y + raw_x + right_y + cond_mid + cond_low + right_mid + right_low:
        c_.wait_send()


N_COPIES = 2 + 6 + 2 + 8 + 4 + 8 + 4


def hand_on(a, b, c, out_a, out_b, out_c, held_a, held_b, held_c, sem):
    ways = ((a, held_a, out_a), (b, held_b, out_b), (c, held_c, out_c))
    copies = [[pltpu.make_async_copy(x, y, sem.at[0, i]), pltpu.make_async_copy(y, z, sem.at[1, i])] for i, (x, y, z) in enumerate(ways)]
    for first, _ in copies:
        first.start()
    for first, second in copies:
        first.wait()
        second.start()
    for _, second in copies:
        second.wait()


def per_device(ngx, ngy, permeability, source, phase_mask):
    vmem = pl.BlockSpec(memory_space=pltpu.VMEM)
    vec = lambda *dims: pltpu.VMEM(dims + (8, 128), F32)
    flat = [x.reshape(512, 128) for x in (permeability, source, phase_mask)]
    fine, mid, low = pl.pallas_call(
        functools.partial(kernel, ngx, ngy),
        out_shape=(
            jax.ShapeDtypeStruct((512, 128), F32),
            jax.ShapeDtypeStruct((16, 8, 64), F32),
            jax.ShapeDtypeStruct((8, 4, 32), F32),
        ),
        in_specs=[pl.BlockSpec(memory_space=pl.ANY)] * 3,
        out_specs=(vmem,) * 3,
        scratch_shapes=[
            vec(ROWS, 4), vec(ROWS, 4),
            vec(16), vec(16), vec(16),
            vec(16), vec(16), vec(ROWS), vec(ROWS),
            vec(ROWS), vec(ROWS), vec(ROWS),
            vec(7, ROWS, 5), vec(ROWS, 5), vec(ROWS, 5),
            vec(MID, 2), vec(MID, 2), vec(2, 2, 4), vec(2, 3, 4), vec(2, 3, 4),
            vec(8, MID, 2), vec(MID, 2), vec(2, MID, 2),
            vec(LOW), vec(7, LOW), vec(LOW), vec(2, LOW),
            pltpu.VMEM((128, 128), F32), pltpu.VMEM((64, 128), F32),
            pltpu.VMEM((512, 128), F32), pltpu.VMEM((512, 128), F32), pltpu.VMEM((512, 128), jnp.int32),
            pltpu.SemaphoreType.DMA((N_COPIES,)), pltpu.SemaphoreType.DMA((N_COPIES,)),
            pltpu.SemaphoreType.DMA((3,)),
        ],
        compiler_params=pltpu.CompilerParams(
            collective_id=0, has_side_effects=True, vmem_limit_bytes=62 * 2**20),
    )(*flat)
    whole = pl.BlockSpec(memory_space=pl.ANY)
    results = (fine, mid, low)
    fine, mid, low = pl.pallas_call(
        hand_on,
        out_shape=tuple(jax.ShapeDtypeStruct(x.shape, F32) for x in results),
        in_specs=[whole] * 3,
        out_specs=(whole,) * 3,
        scratch_shapes=[pltpu.VMEM(x.shape, F32) for x in results] + [pltpu.SemaphoreType.DMA((2, 3))],
        compiler_params=pltpu.CompilerParams(vmem_limit_bytes=62 * 2**20),
    )(*results)
    return fine.reshape(32, 16, 128), mid, low


def solution(mesh):
    placed = (P(None, "gy", "gx"),) * 3
    return jax.shard_map(
        functools.partial(per_device, mesh.shape["gx"], mesh.shape["gy"]),
        mesh=mesh, in_specs=placed, out_specs=placed, check_vma=False)
```

```python
import functools

import jax
import jax.numpy as jnp
from jax import lax
from jax.experimental import pallas as pl
from jax.experimental.pallas import tpu as pltpu
from jax.sharding import PartitionSpec as P

MESH = pl.DeviceIdType.MESH
F32 = jnp.float32
STORAGE = 0.05
LEAK = 0.1
TINY = 1e-30

HALO = 9
ROWS = 16 + 2 * HALO
MID = 24
LOW = 20
MX = 22
LX = 11


def rcp(d):
    r = pl.reciprocal(d, approx=True)
    return r * (2.0 - d * r)


def harm(a, b):
    return (2.0 * a * b) * rcp(jnp.maximum(a + b, TINY))


def lane_of(shape):
    return lax.broadcasted_iota(jnp.int32, shape, len(shape) - 1)


def sub_of(shape):
    return lax.broadcasted_iota(jnp.int32, shape, len(shape) - 2)


def roll(x, shift):
    shift = shift % 128
    return x if shift == 0 else pltpu.roll(x, shift, x.ndim - 1)


def east(x):
    return roll(x, 127)


def west(x):
    return roll(x, 1)


def up(x):
    return pltpu.roll(x, 7, x.ndim - 2)


def down(x):
    return pltpu.roll(x, 1, x.ndim - 2)


def strip_up(x):
    y = roll(x, 96)
    return jnp.where(lane_of(x.shape) >= 96, up(y), y)


def strip_down(x):
    y = roll(x, 32)
    return jnp.where(lane_of(x.shape) < 32, down(y), y)


def groups(parts, shifts):
    lane = lane_of(parts[0].shape)
    out = roll(parts[3], shifts[3])
    for q in (2, 1, 0):
        out = jnp.where(lane < 32 * (q + 1), roll(parts[q], shifts[q]), out)
    return out


def pack_west(m):
    return groups(m, [32 * k + 9 for k in range(4)])


def pack_east(m):
    return groups(m, [32 * k + 23 for k in range(4)])


def main_east(m, k, strip):
    ins = roll(strip, 104 - 32 * k)
    return jnp.where(lane_of(m.shape) == 127, ins, east(m))


def main_west(m, k, strip):
    ins = roll(strip, -(32 * k + 8))
    return jnp.where(lane_of(m.shape) == 0, ins, west(m))


def finish(t, c, store):
    total = t[0]
    for x in t[1:]:
        total = total + x
    return total + store * c + jnp.where(c > 0.0, 0.0, 1.0)


def kernel(ngx, ngy, perm_in, source_in, mask_in, out_fine, out_mid, out_low,
           cm, bm, own_w, own_e, own_b, sr, sl, rl, rr, cs, cse, csw, coef, inv, v,
           cmx, cmid, midx, mrl, mrr, mcoef, mvx, mv, clow, lcoef, lvx, lv, tfine, tmid, tmid64, tlow, perm, source, mask, send, recv, load, store):
    gx, gy = lax.axis_index("gx"), lax.axis_index("gy")
    loads = [pltpu.make_async_copy(a, b, load.at[i])
             for i, (a, b) in enumerate(((perm_in, perm), (mask_in, mask), (source_in, source)))]
    for l in loads:
        l.start()

    def dev(dx, dy):
        return (lax.rem(gx + dx + ngx, ngx), lax.rem(gy + dy + 2 * ngy, ngy))

    around = [(dx, dy) for dx in (-1, 0, 1) for dy in (-1, 0, 1) if (dx, dy) != (0, 0)]
    barrier = pltpu.get_barrier_semaphore()
    for d in around:
        pl.semaphore_signal(barrier, inc=1, device_id=dev(*d), device_id_type=MESH)

    made = [0]

    def copy(src, dst, to):
        i = made[0]
        made[0] += 1
        return pltpu.make_async_remote_copy(
            src_ref=src, dst_ref=dst, send_sem=send.at[i], recv_sem=recv.at[i],
            device_id=dev(*to), device_id_type=MESH)


    def take(ref, y, k):
        return ref[pl.ds(k * 16 + y, 8, stride=64), :]

    lane = lane_of((8, 128))
    c32 = jnp.bitwise_and(lane, 31)
    sub = sub_of((8, 128))
    pair_mid = jnp.clip(2 * (lane - MX), 0, 127)
    pair_low = jnp.clip(2 * lane, 0, 127)

    def compact(x, index):
        return jnp.take_along_axis(x + east(x), index, axis=1, mode="promise_in_bounds")

    for l in loads:
        l.wait()

    def load_pair(i, carry):
        for o in range(2):
            y = 2 * i + o
            conds, rights = [], []
            for k in range(4):
                m = take(mask, y, k)
                c = jnp.where(m == 2, 0.0, take(perm, y, k))
                b = jnp.where(m == 1, take(source, y, k), 0.0)
                cm[HALO + y, k] = c
                bm[HALO + y, k] = b
                conds.append(c)
                rights.append(b)
            aw, ae = pack_west(conds), pack_east(conds)
            bw, be = pack_west(rights), pack_east(rights)
            own_w[y], own_e[y] = aw, ae
            own_b[y] = jnp.where(c32 < 16, bw, be)
            sr[y] = jnp.where(c32 < 16, aw, roll(bw, 16))
            sl[y] = jnp.where(c32 >= 16, ae, roll(be, 112))
        return carry

    def cond_pair(i, carry):
        acc = [None, None]
        for y in (2 * i, 2 * i + 1):
            for k in range(4):
                term = LEAK * take(perm, y, k) + (1.0 - LEAK) * cm[HALO + y, k]
                acc[k // 2] = term if acc[k // 2] is None else acc[k // 2] + term
        for k in range(2):
            cmx[8 + i, k] = compact(acc[k], pair_mid) * 0.125
        return carry

    lax.fori_loop(0, 8, load_pair, 0, unroll=True)

    def mid_pack(src, row0, slot):
        for i in range(4):
            parts = [src[row0 + i + 4 * (q // 2), q % 2] for q in range(4)]
            midx[slot, 0, i] = groups(parts, [32 * q - (MX + 42) for q in range(4)])
            midx[slot, 1, i] = groups(parts, [32 * q - MX for q in range(4)])

    pl.semaphore_wait(barrier, len(around))

    def start(cs_):
        for c_ in cs_:
            c_.start()

    def arrive(cs_):
        for c_ in cs_:
            c_.wait_recv()

    def strips(src_r, src_l, dst_l, dst_r, n):
        own = src_r.shape[0]
        got = []
        for dx, src, dst in ((1, src_r, dst_l), (-1, src_l, dst_r)):
            got.append(copy(src, dst.at[pl.ds(n, own)], (dx, 0)))
            got.append(copy(src.at[pl.ds(own - n, n)], dst.at[pl.ds(0, n)], (dx, 1)))
            got.append(copy(src.at[pl.ds(0, n)], dst.at[pl.ds(n + own, n)], (dx, -1)))
        return got

    def edges(buf, n, own, halo):
        return [copy(buf.at[pl.ds(halo + own - n, n)], buf.at[pl.ds(halo - n, n)], (0, 1)),
                copy(buf.at[pl.ds(halo, n)], buf.at[pl.ds(halo + own, n)], (0, -1))]

    cond_y = edges(cm, HALO, 16, HALO)
    raw_x = strips(sr, sl, rl, rr, HALO)
    right_y = edges(bm, HALO - 1, 16, HALO)
    start(cond_y + raw_x)

    def mid_exchange(buf, slot):
        got = []
        for block, dy in ((0, 1), (2, -1), (1, 0)):
            for dx, side, dst in ((1, 0, mrl), (-1, 1, mrr)):
                got.append(copy(midx.at[slot, side], dst.at[slot, block], (dx, dy)))
        return got[:4] + edges(buf, 8, 8, 8) + got[4:]

    lax.fori_loop(0, 8, cond_pair, 0, unroll=4)
    mid_pack(cmx, 8, 0)
    cond_mid = mid_exchange(cmx, 0)
    start(cond_mid + right_y)

    inside = jnp.where(gx == 0, 9, 0), jnp.where(gx == ngx - 1, 23, 32)
    keep = (c32 >= inside[0]) & (c32 < inside[1])

    def strip_cond(r, aw, ae, live=None):
        c = jnp.where(c32 < 9, rl[r], jnp.where(c32 < 16, aw, jnp.where(c32 < 23, ae, rr[r])))
        c = jnp.where(keep, c, 0.0)
        if live is not None:
            c = c * live
        cs[r] = c
        cse[r] = east(jnp.where(c32 == 16, aw, c))
        csw[r] = west(jnp.where(c32 == 15, ae, c))

    top = sub == 7

    def fine_coefs(r):
        m = [[cm[r + d, k] for k in range(4)] for d in (-1, 0, 1)]
        s = [cs[r + d] for d in (-1, 0, 1)]
        se = cse[r]
        c = s[1]
        te = harm(c, se)
        tw = harm(c, csw[r])
        tn, ts = harm(c, s[2]), harm(c, s[0])
        tu = harm(c, jnp.where(top & (lane >= 96), 0.0, strip_up(c)))
        faces = [te, tw, tn, ts, tu, strip_down(tu)]

        def put(k, faces, c):
            diag = finish(faces, c, STORAGE)
            w = 0.8 * rcp(diag)
            for f in range(6):
                coef[f, r, k] = w * faces[f]
            coef[6, r, k] = w
            inv[r, k] = 1.25 * diag

        put(4, faces, c)
        ups = [harm(m[1][k], m[1][k + 1]) for k in range(3)]
        ups.append(harm(m[1][3], jnp.where(top, 0.0, up(m[1][0]))))
        for k in range(4):
            c = m[1][k]
            e = harm(c, main_east(c, k, s[1]))
            w_ = main_west(e, k, te)
            d_ = ups[k - 1] if k else down(ups[3])
            put(k, [e, w_, harm(c, m[2][k]), harm(c, m[0][k]), ups[k], d_], c)

    def first(r, mid):
        b = [bm[r, k] for k in range(4)]
        b.append(jnp.where(c32 < 9, roll(rl[r], 112), jnp.where(c32 < 23, mid, roll(rr[r], 16))))
        for k in range(5):
            x = coef[6, r, k] * b[k]
            v[r, k] = x
            coef[6, r, k] = x

    def loop(n, unroll):
        def run(body):
            def step(i, carry):
                body(i)
                return carry
            lax.fori_loop(0, n, step, 0, unroll=unroll)
        return run

    arrive([raw_x[0], raw_x[3]])

    @loop(16, True)
    def _(i):
        strip_cond(HALO + i, own_w[i], own_e[i])

    @loop(14, 7)
    def _(i):
        fine_coefs(HALO + 1 + i)

    @loop(14, True)
    def _(i):
        first(HALO + 1 + i, own_b[1 + i])

    arrive(cond_y + raw_x[1:3] + raw_x[4:6])

    @pl.when(gy == 0)
    def _():
        cm[pl.ds(0, HALO)] = jnp.zeros((HALO, 4, 8, 128), F32)

    @pl.when(gy == ngy - 1)
    def _():
        cm[pl.ds(16 + HALO, HALO)] = jnp.zeros((HALO, 4, 8, 128), F32)

    lives = [jnp.where(gy == 0, 0.0, 1.0), jnp.where(gy == ngy - 1, 0.0, 1.0)]

    @loop(HALO, True)
    def _(i):
        for r, live in ((i, lives[0]), (16 + HALO + i, lives[1])):
            parts = [cm[r, k] for k in range(4)]
            strip_cond(r, pack_west(parts), pack_east(parts), live)

    @loop(HALO, 3)
    def _(i):
        for r in (1 + i, 15 + HALO + i):
            fine_coefs(r)

    def mid_join(buf, slot, row):
        block, i = row // 8, row % 8
        out = []
        for k in range(2):
            q = 2 * (i // 4) + k
            left = roll(mrl[slot, block, i % 4], -32 * q)
            right = roll(mrr[slot, block, i % 4], MX + 64 - 32 * q)
            out.append(jnp.where(lane < MX, left, jnp.where(lane < MX + 64, buf[row, k], right)))
        return out

    arrive(cond_mid)
    lo, hi = jnp.where(gx == 0, MX, 0), jnp.where(gx == ngx - 1, MX + 64, 128)
    keep_mid = (lane >= lo) & (lane < hi)

    def join_cond(row):
        joined = mid_join(cmx, 0, row)
        for k in range(2):
            c = jnp.where(keep_mid, joined[k], 0.0)
            cmid[row, k] = c if row // 8 == 1 else c * lives[row // 16]

    def mid_coefs(r):
        x = [[cmid[r + d, k] for k in range(2)] for d in (-1, 0, 1)]
        u = [2.0 * harm(x[1][0], x[1][1]), 2.0 * harm(x[1][1], jnp.where(top, 0.0, up(x[1][0])))]
        for k in range(2):
            c = x[1][k]
            e = 2.0 * harm(c, east(c))
            faces = [e, west(e), 2.0 * harm(c, x[2][k]), 2.0 * harm(c, x[0][k]), u[k], u[0] if k else down(u[1])]
            diag = finish(faces, c, 8.0 * STORAGE)
            w = 0.8 * rcp(diag)
            for f in range(6):
                mcoef[f, r, k] = w * faces[f]
            mcoef[6, r, k] = w
            mcoef[7, r, k] = 1.25 * diag

    for row in range(7, 17):
        join_cond(row)
    for row in range(8, 16):
        mid_coefs(row)

    for i in range(4):
        acc = cmid[8 + 2 * i, 0] + cmid[8 + 2 * i, 1] + cmid[9 + 2 * i, 0] + cmid[9 + 2 * i, 1]
        clow[8 + i] = compact(acc, pair_low) * 0.125

    def low_exchange(buf):
        return [copy(buf.at[pl.ds(8, 4)], buf.at[pl.ds(4, 4)], (0, 1)),
                copy(buf.at[pl.ds(8, 4)], buf.at[pl.ds(12, 4)], (0, -1)),
                copy(buf.at[pl.ds(8, 4)], buf.at[pl.ds(0, 4)], (0, 2)),
                copy(buf.at[pl.ds(8, 4)], buf.at[pl.ds(16, 4)], (0, -2))]

    cond_low = low_exchange(clow)
    start(cond_low)

    arrive(right_y)
    first(HALO, own_b[0])
    first(HALO + 15, own_b[15])

    @loop(HALO - 1, True)
    def _(i):
        for r in (1 + i, 16 + HALO + i):
            parts = [bm[r, k] for k in range(4)]
            first(r, jnp.where(c32 < 16, pack_west(parts), pack_east(parts)))

    def sweep_main(r, k, x, x0, x2, strip):
        u = x[k + 1] if k < 3 else up(x[0])
        d = x[k - 1] if k else down(x[3])
        a = [coef[f, r, k] for f in range(7)]
        return (0.2 * x[k] + a[6] + a[0] * main_east(x[k], k, strip) + a[1] * main_west(x[k], k, strip)
                + a[2] * x2[k] + a[3] * x0[k] + a[4] * u + a[5] * d)

    def row_in(r):
        return [v[r, k] for k in range(5)]

    def sweep_row(r, x0, x, x2):
        s = x[4]
        for k in range(4):
            v[r, k] = sweep_main(r, k, x, x0, x2, s)
        a = [coef[f, r, 4] for f in range(7)]
        v[r, 4] = (0.2 * s + a[6] + a[0] * east(s) + a[1] * west(s) + a[2] * x2[4] + a[3] * x0[4]
                   + a[4] * strip_up(s) + a[5] * strip_down(s))

    def sweep_rows(r0, n, x0, x):
        for o in range(n):
            x2 = row_in(r0 + o + 1)
            sweep_row(r0 + o, x0, x, x2)
            x0, x = x, x2
        return x0, x

    for j in range(1, 8):
        sweep_rows(j + 1, ROWS - 2 - 2 * j, row_in(j), row_in(j + 1))

    def fine_residual(i, carry):
        acc = [None, None]
        r0 = HALO + 2 * i
        rows = [[v[r0 + o - 1, k] for k in range(4)] for o in range(4)]
        for o in range(2):
            r = r0 + o
            x0, x, x2 = rows[o], rows[o + 1], rows[o + 2]
            strip = v[r, 4]
            for k in range(4):
                res = (sweep_main(r, k, x, x0, x2, strip) - x[k]) * inv[r, k]
                acc[k // 2] = res if acc[k // 2] is None else acc[k // 2] + res
        for k in range(2):
            mvx[8 + i, k] = mcoef[6, 8 + i, k] * compact(acc[k], pair_mid)
        return carry

    lax.fori_loop(0, 8, fine_residual, 0, unroll=4)
    mid_pack(mvx, 8, 1)
    right_mid = mid_exchange(mvx, 1)
    start(right_mid)

    for row in list(range(7)) + list(range(17, MID)):
        join_cond(row)
    for row in list(range(1, 8)) + list(range(16, MID - 1)):
        mid_coefs(row)

    def write_fine(y, carry):
        for k in range(4):
            tfine[pl.ds(k * 16 + y, 8, stride=64), :] = v[HALO + y, k]
        return carry

    lax.fori_loop(0, 16, write_fine, 0, unroll=True)
    stores = [pltpu.make_async_copy(tfine, out_fine, store.at[0]), pltpu.make_async_copy(tmid64, out_mid, store.at[1])]
    stores[0].start()

    arrive(cond_low)
    for row in list(range(1, 8)) + list(range(12, 19)):
        far = ngy - 1 - gy if row >= 12 else gy
        near = (row - 12) // 4 + 1 if row >= 12 else (11 - row) // 4
        clow[row] = clow[row] * jnp.where(far < near, 0.0, 1.0)

    for r in range(2, 18):
        c = clow[r]
        u = 4.0 * harm(c, jnp.where(top, 0.0, up(c)))
        e = 4.0 * harm(c, east(c))
        faces = [e, west(e), 4.0 * harm(c, clow[r + 1]), 4.0 * harm(c, clow[r - 1]), u, down(u)]
        diag = finish(faces, c, 64.0 * STORAGE)
        w = 0.8 * rcp(diag)
        for f in range(6):
            lcoef[f, r] = w * faces[f]
        lcoef[6, r] = w

    arrive(right_mid)
    for row in range(MID):
        joined = mid_join(mvx, 1, row)
        for k in range(2):
            mv[0, row, k] = joined[k]
            mcoef[6, row, k] = joined[k]

    def mid_sweep(p, r):
        x0, x, x2 = ([mv[p, r + d, k] for k in range(2)] for d in (-1, 0, 1))
        out = []
        for k in range(2):
            a = [mcoef[f, r, k] for f in range(7)]
            u = x[1] if k == 0 else up(x[0])
            d = x[0] if k else down(x[1])
            out.append(0.2 * x[k] + a[6] + a[0] * east(x[k]) + a[1] * west(x[k]) + a[2] * x2[k] + a[3] * x0[k]
                       + a[4] * u + a[5] * d)
        return x, out

    for j in range(1, 8):
        p, q = (j + 1) % 2, j % 2
        for r in range(j, MID - j):
            _, new = mid_sweep(p, r)
            for k in range(2):
                mv[q, r, k] = new[k]

    for i in range(4):
        acc = None
        for o in range(2):
            r = 8 + 2 * i + o
            x, new = mid_sweep(1, r)
            for k in range(2):
                res = (new[k] - x[k]) * mcoef[7, r, k]
                acc = res if acc is None else acc + res
        lvx[8 + i] = lcoef[6, 8 + i] * compact(acc, pair_low)
    right_low = low_exchange(lvx)
    start(right_low)

    for i in range(8):
        for k in range(2):
            tmid[pl.ds(k * 8 + i, 8, stride=16), :] = roll(mv[1, 8 + i, k], -MX)
    tmid64[...] = tmid[...].reshape(16, 8, 128)[:, :, :64]
    stores[1].start()

    arrive(right_low)
    for j in range(1, 8):
        src, q = lvx if j == 1 else lv.at[(j + 1) % 2], j % 2
        for r in range(1 + j, LOW - 1 - j):
            x = src[r]
            a = [lcoef[f, r] for f in range(6)]
            lv[q, r] = (0.2 * x + lvx[r] + a[0] * east(x) + a[1] * west(x) + a[2] * src[r + 1] + a[3] * src[r - 1]
                        + a[4] * up(x) + a[5] * down(x))
    for i in range(4):
        tlow[pl.ds(i, 8, stride=8), :] = roll(lv[1, 8 + i], -LX)
    out_low[...] = tlow[...].reshape(8, 8, 128)[:, :4, :32]

    for c_ in stores:
        c_.wait()
    for c_ in cond_y + raw_x + right_y + cond_mid + cond_low + right_mid + right_low:
        c_.wait_send()


N_COPIES = 2 + 6 + 2 + 8 + 4 + 8 + 4


PIECES = 4


def hand_on(a, b, c, out_a, out_b, out_c, held_a, held_b, held_c, sem):
    n = a.shape[0] // PIECES
    ways = [tuple(x.at[pl.ds(n * i, n)] for x in (a, held_a, out_a)) for i in range(PIECES)]
    ways += [(b, held_b, out_b), (c, held_c, out_c)]
    copies = [(pltpu.make_async_copy(x, y, sem.at[0, i]), pltpu.make_async_copy(y, z, sem.at[1, i]))
              for i, (x, y, z) in enumerate(ways)]
    for first, _ in copies:
        first.start()
    for first, second in copies:
        first.wait()
        second.start()
    for _, second in copies:
        second.wait()


def per_device(ngx, ngy, permeability, source, phase_mask):
    vmem = pl.BlockSpec(memory_space=pltpu.VMEM)
    vec = lambda *dims: pltpu.VMEM(dims + (8, 128), F32)
    flat = [x.reshape(512, 128) for x in (permeability, source, phase_mask)]
    fine, mid, low = pl.pallas_call(
        functools.partial(kernel, ngx, ngy),
        out_shape=(
            jax.ShapeDtypeStruct((512, 128), F32),
            jax.ShapeDtypeStruct((16, 8, 64), F32),
            jax.ShapeDtypeStruct((8, 4, 32), F32),
        ),
        in_specs=[pl.BlockSpec(memory_space=pl.ANY)] * 3,
        out_specs=(pl.BlockSpec(memory_space=pl.ANY),) * 2 + (vmem,),
        scratch_shapes=[
            vec(ROWS, 4), vec(ROWS, 4),
            vec(16), vec(16), vec(16),
            vec(16), vec(16), vec(ROWS), vec(ROWS),
            vec(ROWS), vec(ROWS), vec(ROWS),
            vec(7, ROWS, 5), vec(ROWS, 5), vec(ROWS, 5),
            vec(MID, 2), vec(MID, 2), vec(2, 2, 4), vec(2, 3, 4), vec(2, 3, 4),
            vec(8, MID, 2), vec(MID, 2), vec(2, MID, 2),
            vec(LOW), vec(7, LOW), vec(LOW), vec(2, LOW),
            pltpu.VMEM((512, 128), F32), pltpu.VMEM((128, 128), F32),
            pltpu.VMEM((16, 8, 64), F32), pltpu.VMEM((64, 128), F32),
            pltpu.VMEM((512, 128), F32), pltpu.VMEM((512, 128), F32), pltpu.VMEM((512, 128), jnp.int32),
            pltpu.SemaphoreType.DMA((N_COPIES,)), pltpu.SemaphoreType.DMA((N_COPIES,)),
            pltpu.SemaphoreType.DMA((3,)), pltpu.SemaphoreType.DMA((2,)),
        ],
        compiler_params=pltpu.CompilerParams(
            collective_id=0, has_side_effects=True, vmem_limit_bytes=62 * 2**20),
    )(*flat)
    whole = pl.BlockSpec(memory_space=pl.ANY)
    results = (fine, mid, low)
    fine, mid, low = pl.pallas_call(
        hand_on,
        out_shape=tuple(jax.ShapeDtypeStruct(x.shape, F32) for x in results),
        in_specs=[whole] * 3,
        out_specs=(whole,) * 3,
        scratch_shapes=[pltpu.VMEM(x.shape, F32) for x in results] + [pltpu.SemaphoreType.DMA((2, PIECES + 2))],
        compiler_params=pltpu.CompilerParams(vmem_limit_bytes=62 * 2**20),
    )(*results)
    return fine.reshape(32, 16, 128), mid, low


def solution(mesh):
    placed = (P(None, "gy", "gx"),) * 3
    return jax.shard_map(
        functools.partial(per_device, mesh.shape["gx"], mesh.shape["gy"]),
        mesh=mesh, in_specs=placed, out_specs=placed, check_vma=False)
```
